128 devices in a mesh: lev: 2 (over y_hi), horiz: 64 (over x, y_lo, z, core).
Axes of the slice: x: 4, y: 4 (y_hi: 2, y_lo: 2; y = y_hi * 2 + y_lo), z: 4, core: 2. Of those that a mesh axis runs over, the one named last changes fastest.
Arguments:
- concentration: bfloat16 [12, 128, 32, 8192], P('lev', 'horiz'), may hold values from 0.049804688 to 1
- flow_planes: float32 [2, 12, 128, 8192], P(None, None, 'lev', 'horiz'), may hold values from 0.5 to 2
- agg_kernel: bfloat16 [1024, 32], replicated, may hold values from -0.1875 to 0.1875
- settle_rate: float32 [32], replicated, may hold values from 0.05 to 4
- wet_mask: int32 [128, 8192], P('horiz'), may hold values 0 or 1
- bed_level: int32 [128, 8192], P('horiz'), may hold values from 0 to 11
Outputs:
- floc: bfloat16 [12, 128, 32, 8192], P('lev', 'horiz')
- near_bed: float32 [128, 32, 8192], P('lev', None, 'horiz')
The draws below stay inside these ranges and needn't reach their ends.
All inputs are finite; a program needn't handle non-finite values. No bound on the sum of `wet_mask` on one device may be relied on, other than what follows from the above.
Results may differ from the reference program's by a relative error of at most 0.0023.
Values sent between devices are 32-bit elements; how exact they have to be, the bound alone decides.
No kernel may reach another device: no remote copies, remote signals or barrier semaphores. Data moves between devices by JAX's collectives and lax.ppermute only.
A program may use at most 256 MiB of HBM per device.

```python
import math
from functools import partial
import jax
import jax.numpy as jnp
from jax import lax

CLASSES = 32
PAIRS = 1024
LEVELS = 12
NX = 128
NY = 8192


def touch_ends(result, key, smallest, top_value):
    longest = result.shape.index(max(result.shape))
    spots = []
    for shift in (0, 1):
        where = [jax.random.randint(jax.random.fold_in(key, axis), (), 0, length) for axis, length in enumerate(result.shape)]
        where[longest] = (where[longest] + shift) % result.shape[longest]
        spots.append(tuple(where))
    return result.at[spots[0]].set(smallest).at[spots[1]].set(top_value)


def level_of(stream_key, extent, pieces, least, top_value):
    level = 1.0
    for dim, parts in pieces:
        heights = jax.random.uniform(jax.random.fold_in(jax.random.fold_in(stream_key, 6), dim), (parts,), jnp.float32, least / len(pieces), top_value / len(pieces))
        level = level * jnp.repeat(jnp.exp(heights), extent[dim] // parts).reshape((-1,) + (1,) * (len(extent) - 1 - dim))
    return level


def normal_values(own_key, shape, scale, most, held_as=jnp.bfloat16):
    drawn = jax.random.normal(own_key, shape, jnp.float32) * scale
    return jnp.minimum(jnp.maximum(drawn, -most), most).astype(held_as)


def setup_inputs(seed: int = 0) -> dict:
    keys = jax.random.split(jax.random.key(seed), 7)
    concentration = jnp.clip(jnp.exp(math.log(1.0) - 2.9996462 * jax.random.uniform(keys[0], (LEVELS, NX, CLASSES, NY), jnp.float32) ** level_of(keys[0], (LEVELS, NX, CLASSES, NY), ((0, 2), (1, 64)), -0.2, 0.2)), 0.049804688, 1.0).astype(jnp.bfloat16)
    flow_planes = jnp.clip(jnp.exp(math.log(2.0) - 1.3862944 * jax.random.uniform(keys[1], (2, LEVELS, NX, NY), jnp.float32) ** level_of(keys[1], (2, LEVELS, NX, NY), ((2, 2), (3, 64)), -0.2, 0.2)), 0.5, 2.0)
    agg_kernel = normal_values(keys[2], (PAIRS, CLASSES), PAIRS ** -0.5, 0.1875)
    settle_rate = jnp.clip(jnp.exp(jax.random.uniform(keys[3], (CLASSES,), jnp.float32, math.log(0.05), math.log(4.0))), 0.05, 4.0)
    wet_mask = touch_ends((jax.random.randint(keys[4], (NX, NY), 0, 4) < 3).astype(jnp.int32), jax.random.fold_in(keys[4], 1), 0, 1)
    bed_level = touch_ends(jax.random.randint(keys[5], (NX, NY), 0, LEVELS), jax.random.fold_in(keys[5], 1), 0, LEVELS - 1).astype(jnp.int32)
    return {"concentration": concentration, "flow_planes": flow_planes, "agg_kernel": agg_kernel, "settle_rate": settle_rate, "wet_mask": wet_mask, "bed_level": bed_level}


def aggregate(agg_kernel, operands):
    block, stir = operands
    floc_block = block.astype(jnp.float32)
    classes = floc_block.shape[0]
    pairs = (floc_block[:, None, :] * floc_block[None, :, :]).reshape(classes * classes, floc_block.shape[1]).astype(jnp.bfloat16)
    change = lax.dot_general(agg_kernel, pairs, (((0,), (0,)), ((), ())), preferred_element_type=jnp.float32)
    return floc_block + stir[None, :] * change


def coefficients(thickness, level_ids, wet, bed_level, settle_rate):
    above = (level_ids[:, None, None] <= bed_level[None]).astype(jnp.float32)
    speed_ratio = wet[None, :, None, :] * settle_rate[None, None, :, None] / thickness[:, :, None, :]
    return above[:, :, None, :], speed_ratio


def reference(concentration, flow_planes, agg_kernel, settle_rate, wet_mask, bed_level):
    levels, grid_rows, classes, width = concentration.shape
    shear_rate = flow_planes[0]
    thickness = flow_planes[1]
    wet = wet_mask.astype(jnp.float32)
    stirring = (wet[None] * shear_rate).reshape(levels * grid_rows, width)
    aggregated = lax.map(partial(aggregate, agg_kernel), (concentration.reshape(levels * grid_rows, classes, width), stirring))
    aggregated = aggregated.reshape(levels, grid_rows, classes, width)
    level_ids = jnp.arange(levels, dtype=jnp.int32)

    def settle(carry, operands):
        inflow, near_total = carry
        level_aggr, level_thick, level_index = operands
        above, speed_ratio = coefficients(level_thick[None], level_index[None], wet, bed_level, settle_rate)
        keep = above[0] * (speed_ratio[0] / (1.0 + speed_ratio[0]))
        fresh = above[0] * (level_aggr / (1.0 + speed_ratio[0]))
        inflow = keep * inflow + fresh
        at_bed = (level_index == bed_level).astype(jnp.float32)
        near_total = near_total + inflow * at_bed[:, None, :]
        return (inflow, near_total), inflow

    start = jnp.zeros((grid_rows, classes, width), jnp.float32)
    (last_inflow, near_bed), settled = lax.scan(settle, (start, start), (aggregated, thickness, level_ids))
    return settled.astype(jnp.bfloat16), near_bed
```

```python
from functools import partial

import jax
import jax.numpy as jnp
from jax import lax
from jax.experimental import pallas as pl
from jax.experimental.pallas import tpu as pltpu
from jax.sharding import PartitionSpec as P

LANES = 128
F32 = jnp.float32
BF16 = jnp.bfloat16
VMEM_BYTES = 48 << 20


def pair_weights(agg_kernel, classes):
    half = classes // 2
    whole = agg_kernel.astype(F32).reshape(classes, classes, classes).transpose(2, 0, 1)
    first = whole[:, :half, :half]
    cross = whole[:, :half, half:] + whole[:, half:, :half].transpose(0, 2, 1)
    last = whole[:, half:, half:]
    top = jnp.concatenate([first, cross], axis=2).reshape(classes, half * classes)
    rows = jnp.concatenate([top, last.reshape(classes, half * half)], axis=1)
    high = lax.reduce_precision(rows, 8, 7)
    return jnp.concatenate([high, rows - high], axis=0).astype(BF16)


def change_body(step, weight_ref, conc_ref, change_ref):
    classes, width = conc_ref.shape[2:]
    half = classes // 2
    for start in range(0, width, step):
        cols = slice(start, start + step)
        conc = conc_ref[0, 0, :, cols]
        pairs = []
        for one in range(classes):
            low = 0 if one < half else half
            pairs.append(conc[low:] * jnp.broadcast_to(conc[one : one + 1], (classes - low, step)))
        both = lax.dot_general(
            weight_ref[...],
            jnp.concatenate(pairs, axis=0),
            (((1,), (0,)), ((), ())),
            preferred_element_type=F32,
        )
        change_ref[0, 0, :, cols] = both[:classes] + both[classes:]


def change_of(weights, conc):
    depth, rows, classes, width = conc.shape
    pairs = weights.shape[1]
    return pl.pallas_call(
        partial(change_body, min(width, 2048)),
        out_shape=jax.ShapeDtypeStruct(conc.shape, F32),
        grid=(depth, rows),
        in_specs=[
            pl.BlockSpec(weights.shape, lambda k, x: (0, 0)),
            pl.BlockSpec((1, 1, classes, width), lambda k, x: (k, x, 0, 0)),
        ],
        out_specs=pl.BlockSpec((1, 1, classes, width), lambda k, x: (k, x, 0, 0)),
        compiler_params=pltpu.CompilerParams(vmem_limit_bytes=VMEM_BYTES),
        cost_estimate=pl.CostEstimate(
            flops=2 * weights.shape[0] * pairs * depth * rows * width,
            bytes_accessed=6 * conc.size,
            transcendentals=0,
        ),
        name="change",
    )(weights, conc)


def reciprocal(x):
    rough = pl.reciprocal(x, approx=True)
    return rough * (2.0 - x * rough)


def settle_rows(place_ref, conc_ref, change_ref, flow_ref, rate_ref, wet_ref, bed_ref, start, emit):
    depth, rows, classes, width = conc_ref.shape
    first_level = place_ref[0] * depth
    for tile in range(width // LANES):
        cols = slice(tile * LANES, (tile + 1) * LANES)
        for x in range(rows):
            wet = wet_ref[x : x + 1, cols].astype(F32)
            bed = jnp.broadcast_to(bed_ref[x : x + 1, cols] - first_level, (classes, LANES))
            speed = wet * rate_ref[...]
            carry = start(tile, x)
            for k in range(depth):
                shear = flow_ref[tile, k * rows + x : k * rows + x + 1, :]
                at = (depth + k) * rows + x
                thick = flow_ref[tile, at : at + 1, :]
                change = change_ref[k, x, :, cols]
                aggregated = conc_ref[k, x, :, cols].astype(F32) + (wet * shear) * change
                settled = (speed * carry + thick * aggregated) * reciprocal(thick + speed)
                above = k <= bed
                carry = jnp.where(above, settled, carry)
                emit(tile, x, k, above, carry)


def flux_body(place_ref, conc_ref, change_ref, flow_ref, rate_ref, wet_ref, bed_ref, flux_ref, sent_ref):
    rows, classes = conc_ref.shape[1:3]
    depth = conc_ref.shape[0]
    zero = jnp.zeros((classes, LANES), F32)

    def emit(tile, x, k, above, carry):
        if k == depth - 1:
            part = slice(x * classes, (x + 1) * classes)
            flux_ref[tile, part, :] = carry
            sent_ref[tile, part, :] = carry

    settle_rows(
        place_ref, conc_ref, change_ref, flow_ref, rate_ref, wet_ref, bed_ref, lambda tile, x: zero, emit
    )
    top = rows * classes
    for tile in range(flux_ref.shape[0]):
        cols = slice(tile * LANES, (tile + 1) * LANES)
        wet = wet_ref[:, cols].astype(F32)
        bed = bed_ref[:, cols].astype(F32)
        pad = jnp.zeros((sent_ref.shape[1] - top - 2 * rows, LANES), F32)
        sent_ref[tile, top:, :] = jnp.concatenate([wet, bed, pad], axis=0)


def floc_body(place_ref, conc_ref, change_ref, flow_ref, rate_ref, wet_ref, bed_ref, inflow_ref, floc_ref):
    classes = conc_ref.shape[2]

    def start(tile, x):
        return inflow_ref[tile, x * classes : (x + 1) * classes, :]

    def emit(tile, x, k, above, carry):
        cols = slice(tile * LANES, (tile + 1) * LANES)
        floc_ref[k, x, :, cols] = jnp.where(above, carry, 0.0).astype(BF16)

    settle_rows(place_ref, conc_ref, change_ref, flow_ref, rate_ref, wet_ref, bed_ref, start, emit)


def settle_call(body, name, place, operands, inflow, out_shape, out_specs, tiles):
    conc, change, flow, rate, wet, bed = operands
    depth, rows, classes, width = conc.shape
    cols = tiles * LANES
    steps = width // cols
    block = pl.BlockSpec((depth, rows, classes, cols), lambda i, place: (0, 0, 0, i))
    in_specs = [
        block,
        block,
        pl.BlockSpec((tiles,) + flow.shape[1:], lambda i, place: (place[1] * steps + i, 0, 0)),
        pl.BlockSpec(rate.shape, lambda i, place: (0, 0)),
        pl.BlockSpec((rows, cols), lambda i, place: (0, i)),
        pl.BlockSpec((rows, cols), lambda i, place: (0, i)),
    ]
    args = [conc, change, flow, rate, wet, bed]
    if inflow is not None:
        in_specs.append(pl.BlockSpec((tiles,) + inflow.shape[1:], lambda i, place: (i, 0, 0)))
        args.append(inflow)
    return pl.pallas_call(
        body,
        out_shape=out_shape,
        grid_spec=pltpu.PrefetchScalarGridSpec(
            num_scalar_prefetch=1, grid=(steps,), in_specs=in_specs, out_specs=out_specs
        ),
        compiler_params=pltpu.CompilerParams(vmem_limit_bytes=VMEM_BYTES),
        cost_estimate=pl.CostEstimate(
            flops=12 * conc.size, bytes_accessed=8 * conc.size, transcendentals=conc.size
        ),
        name=name,
    )(place, *args)


def through_body(place_ref, flow_ref, marks_ref, rate_ref, through_ref):
    levels = flow_ref.shape[1]
    sources = marks_ref.shape[0]
    rows = through_ref.shape[0] // sources
    shape = through_ref.shape[1:]
    for source in range(sources):
        for x in range(rows):
            row = source * rows + x
            speed = marks_ref[source, x : x + 1, :] * rate_ref[...]
            bed = jnp.broadcast_to(marks_ref[source, rows + x : rows + x + 1, :], shape)
            through = jnp.ones(shape, F32)
            for k in range(levels):
                thick = flow_ref[0, k, row : row + 1, :]
                keep = speed * reciprocal(thick + speed)
                through = jnp.where(bed >= float(levels + k), through * keep, through)
            through_ref[row] = through


def near_body(place_ref, through_ref, own_ref, other_ref, near_ref):
    sources = own_ref.shape[0]
    classes = through_ref.shape[1]
    rows = through_ref.shape[0] // sources
    is_upper = place_ref[0] == 0
    for source in range(sources):
        for x in range(rows):
            part = slice(x * classes, (x + 1) * classes)
            own = own_ref[source, part, :]
            other = other_ref[source, part, :]
            upper = jnp.where(is_upper, own, other)
            lower = jnp.where(is_upper, other, own)
            near_ref[source * rows + x] = through_ref[source * rows + x] * upper + lower


def local(concentration, flow_planes, agg_kernel, settle_rate, wet_mask, bed_level):
    depth, rows, classes, width = concentration.shape
    planes, levels, tall, _ = flow_planes.shape
    groups, spread = lax.axis_size("lev"), lax.axis_size("horiz")
    lev, horiz = lax.axis_index("lev"), lax.axis_index("horiz")
    share = spread // groups
    place = jnp.stack([lev, horiz // share]).astype(jnp.int32)
    rate = jnp.broadcast_to(settle_rate[:, None], (classes, LANES))

    slots = flow_planes.reshape(planes, groups, depth, share, rows, LANES).transpose(1, 3, 0, 2, 4, 5)
    slots = jnp.broadcast_to(slots[:, None], (groups, groups) + slots.shape[1:])
    slots = slots.reshape(groups * spread, planes * depth * rows, LANES)
    flow = lax.all_to_all(slots, ("lev", "horiz"), split_axis=0, concat_axis=0, tiled=True)

    change = change_of(pair_weights(agg_kernel, classes), concentration)

    operands = (concentration, change, flow, rate, wet_mask, bed_level)
    tiles = 8
    held = rows * classes
    marked = held + 8 * pl.cdiv(2 * rows, 8)
    flux, sent = settle_call(
        flux_body,
        "flux",
        place,
        operands,
        None,
        (
            jax.ShapeDtypeStruct((spread, held, LANES), F32),
            jax.ShapeDtypeStruct((spread, marked, LANES), F32),
        ),
        (
            pl.BlockSpec((tiles, held, LANES), lambda i, place: (i, 0, 0)),
            pl.BlockSpec((tiles, marked, LANES), lambda i, place: (i, 0, 0)),
        ),
        tiles,
    )
    inflow = lax.ppermute(flux, "lev", [(0, 1)])
    spread_out = lax.all_to_all(sent, "horiz", split_axis=0, concat_axis=0, tiled=True)
    away = lax.dynamic_slice(spread_out, ((1 - lev) * share, 0, 0), (share, held, LANES))
    other = lax.ppermute(away, "lev", [(0, 1), (1, 0)])

    floc = settle_call(
        floc_body,
        "floc",
        place,
        operands,
        inflow,
        jax.ShapeDtypeStruct(concentration.shape, BF16),
        pl.BlockSpec((depth, rows, classes, tiles * LANES), lambda i, place: (0, 0, 0, i)),
        tiles,
    )

    near_shape = (tall, classes, LANES)
    some = 8
    steps = share // some
    near_block = pl.BlockSpec((some * rows, classes, LANES), lambda i, place: (i, 0, 0))
    through = pl.pallas_call(
        through_body,
        out_shape=jax.ShapeDtypeStruct(near_shape, F32),
        grid_spec=pltpu.PrefetchScalarGridSpec(
            num_scalar_prefetch=1,
            grid=(steps,),
            in_specs=[
                pl.BlockSpec((1, depth, some * rows, LANES), lambda i, place: (1, 1, i, 0)),
                pl.BlockSpec(
                    (some, marked - held, LANES),
                    lambda i, place: (place[0] * steps + i, held // (marked - held), 0),
                ),
                pl.BlockSpec(rate.shape, lambda i, place: (0, 0)),
            ],
            out_specs=near_block,
        ),
        cost_estimate=pl.CostEstimate(
            flops=8 * depth * tall * classes * LANES,
            bytes_accessed=8 * tall * classes * LANES,
            transcendentals=depth * tall * classes * LANES,
        ),
        name="through",
    )(place, flow_planes, spread_out, rate)
    near_bed = pl.pallas_call(
        near_body,
        out_shape=jax.ShapeDtypeStruct(near_shape, F32),
        grid_spec=pltpu.PrefetchScalarGridSpec(
            num_scalar_prefetch=1,
            grid=(steps,),
            in_specs=[
                near_block,
                pl.BlockSpec((some, held, LANES), lambda i, place: (place[0] * steps + i, 0, 0)),
                pl.BlockSpec((some, held, LANES), lambda i, place: (i, 0, 0)),
            ],
            out_specs=near_block,
        ),
        cost_estimate=pl.CostEstimate(
            flops=2 * tall * classes * LANES,
            bytes_accessed=16 * tall * classes * LANES,
            transcendentals=0,
        ),
        name="near",
    )(place, through, spread_out, other)
    return (floc, near_bed)


def solution(mesh):
    in_specs = (
        P("lev", "horiz", None, None),
        P(None, None, "lev", "horiz"),
        P(),
        P(),
        P("horiz", None),
        P("horiz", None),
    )
    out_specs = (P("lev", "horiz", None, None), P("lev", None, "horiz"))
    return jax.shard_map(local, mesh=mesh, in_specs=in_specs, out_specs=out_specs, check_vma=False)
```

```python
from functools import partial

import jax
import jax.numpy as jnp
import numpy as np
from jax import lax
from jax.experimental import pallas as pl
from jax.experimental.pallas import tpu as pltpu
from jax.sharding import PartitionSpec as P

LANES = 128
BESIDE = 8
F32 = jnp.float32
BF16 = jnp.bfloat16
VMEM_BYTES = 56 << 20


def pair_order(classes):
    half = classes // 2
    order = [(one, half + two) for one in range(half) for two in range(half)]
    for base in (0, half):
        for shift in range(half // 2):
            order += [(base + one, base + (one + shift) % half) for one in range(half)]
    for base in (0, half):
        order += [(base + one, base + one + half // 2) for one in range(half // 2)]
    return order


def pair_weights(agg_kernel, classes):
    order = pair_order(classes)
    chosen = np.zeros((classes * classes, len(order)), np.float32)
    for place, (one, two) in enumerate(order):
        chosen[one * classes + two, place] = 1.0
        chosen[two * classes + one, place] = 1.0
    rows = lax.dot_general(
        agg_kernel, jnp.asarray(chosen, BF16), (((0,), (0,)), ((), ())), preferred_element_type=F32
    )
    high = lax.reduce_precision(rows, 8, 7)
    return jnp.concatenate([high, rows - high], axis=0).astype(BF16)


def pair_rows(conc):
    half = conc.shape[0] // 2
    quarter = half // 2
    halves = [conc[:half], conc[half:]]
    wide = [part.astype(F32) for part in halves]
    pairs = [
        halves[1] * jnp.broadcast_to(conc[one : one + 1], halves[1].shape) for one in range(half)
    ]
    for part, whole in zip(halves, wide):
        pairs.append(part * part)
        for shift in range(1, quarter):
            pairs.append(part * pltpu.roll(whole, half - shift, axis=0).astype(BF16))
    last = [whole[:quarter] * whole[quarter:] for whole in wide]
    pairs.append(jnp.concatenate(last, axis=0).astype(BF16))
    return jnp.concatenate(pairs, axis=0)


def change_body(step, weight_ref, conc_ref, change_ref):
    classes, width = conc_ref.shape[2:]
    for start in range(0, width, step):
        cols = slice(start, start + step)
        both = lax.dot_general(
            weight_ref[...],
            pair_rows(conc_ref[0, 0, :, cols]),
            (((1,), (0,)), ((), ())),
            preferred_element_type=F32,
        )
        change_ref[0, 0, :, cols] = both[:classes] + both[classes:]


def change_of(weights, conc):
    depth, rows, classes, width = conc.shape
    return pl.pallas_call(
        partial(change_body, min(width, 2048)),
        out_shape=jax.ShapeDtypeStruct(conc.shape, F32),
        grid=(depth, rows),
        in_specs=[
            pl.BlockSpec(weights.shape, lambda k, x: (0, 0)),
            pl.BlockSpec((1, 1, classes, width), lambda k, x: (k, x, 0, 0)),
        ],
        out_specs=pl.BlockSpec((1, 1, classes, width), lambda k, x: (k, x, 0, 0)),
        compiler_params=pltpu.CompilerParams(vmem_limit_bytes=VMEM_BYTES),
        cost_estimate=pl.CostEstimate(
            flops=2 * weights.size * depth * rows * width,
            bytes_accessed=6 * conc.size,
            transcendentals=0,
        ),
        name="change",
    )(weights, conc)


def reciprocal(x):
    rough = pl.reciprocal(x, approx=True)
    return rough * (2.0 - x * rough)


def settle_block(xs, first_level, chunk, conc_ref, change_ref, flow_ref, rate_ref, wet_ref, bed_ref, start, emit):
    _, depth, _, classes, width = conc_ref.shape
    rows = wet_ref.shape[1]
    for tile in range(width // LANES):
        cols = slice(tile * LANES, (tile + 1) * LANES)
        for n, x in enumerate(xs):
            wet = wet_ref[chunk, x : x + 1, cols].astype(F32)
            bed = jnp.broadcast_to(bed_ref[chunk, x : x + 1, cols] - first_level, (classes, LANES))
            speed = wet * rate_ref[...]
            carry = start(tile, n)
            for k in range(depth):
                shear = flow_ref[chunk, tile, k * rows + x : k * rows + x + 1, :]
                at = (depth + k) * rows + x
                thick = flow_ref[chunk, tile, at : at + 1, :]
                change = change_ref[chunk, k, n, :, cols]
                aggregated = conc_ref[chunk, k, n, :, cols].astype(F32) + (wet * shear) * change
                settled = (speed * carry + thick * aggregated) * reciprocal(thick + speed)
                above = k <= bed
                carry = jnp.where(above, settled, carry)
                emit(tile, n, k, above, carry)


def chunk_copies(xs, place_ref, hbm, held, sems, chunk):
    chunks = held[0].shape[0]
    width = held[0].shape[-1]
    tiles = held[2].shape[1]
    cols = pl.ds(chunk * width, width)
    some = pl.ds(xs[0], len(xs))
    parts = [
        hbm[0].at[:, some, :, cols],
        hbm[1].at[:, some, :, cols],
        hbm[2].at[pl.ds(place_ref[1] * (chunks * tiles) + chunk * tiles, tiles)],
        hbm[3].at[:, cols],
        hbm[4].at[:, cols],
    ]
    if len(held) > 5:
        parts.append(hbm[5].at[pl.ds(chunk * tiles, tiles)])
    return [
        pltpu.make_async_copy(part, held[at].at[chunk], sems.at[at, chunk])
        for at, part in enumerate(parts)
    ]


def flux_body(xs, place_ref, rate_ref, *refs):
    hbm, flux_hbm, sent_hbm, held = refs[:5], refs[5:7], refs[7], refs[8:13]
    value_ref, marks_ref, in_sems, out_sems = refs[13:]
    chunks, depth, rows, classes, _ = held[0].shape
    tiles = held[2].shape[1]
    for chunk in range(chunks):
        for copy in chunk_copies(xs, place_ref, hbm, held, in_sems, chunk):
            copy.start()
    zero = jnp.zeros((classes, LANES), F32)
    turned = jnp.where(place_ref[0] == place_ref[1], 0, 1)

    def sends(chunk):
        here = pl.ds(chunk * tiles, tiles)
        to = pl.ds(jnp.bitwise_xor(chunk, turned) * tiles, tiles)
        top = rows * classes
        copies = [
            pltpu.make_async_copy(
                value_ref.at[chunk, :, pl.ds(n * classes, classes)], part.at[here], out_sems.at[n, chunk]
            )
            for n, part in enumerate(flux_hbm)
        ]
        copies.append(
            pltpu.make_async_copy(
                value_ref.at[chunk], sent_hbm.at[to, pl.ds(0, top)], out_sems.at[2, chunk]
            )
        )
        copies.append(
            pltpu.make_async_copy(
                marks_ref.at[chunk], sent_hbm.at[to, pl.ds(top, marks_ref.shape[2])], out_sems.at[3, chunk]
            )
        )
        return copies

    def step(chunk, _):
        for copy in chunk_copies(xs, place_ref, hbm, held, in_sems, chunk):
            copy.wait()

        def emit(tile, n, k, above, carry):
            if k == depth - 1:
                value_ref[chunk, tile, n * classes : (n + 1) * classes, :] = carry

        settle_block(
            xs, place_ref[0] * depth, chunk, *held[:3], rate_ref, *held[3:], lambda tile, n: zero, emit
        )
        for tile in range(tiles):
            cols = slice(tile * LANES, (tile + 1) * LANES)
            wet = held[3][chunk, :, cols].astype(F32)
            bed = held[4][chunk, :, cols].astype(F32)
            pad = jnp.zeros((marks_ref.shape[2] - 2 * rows, LANES), F32)
            marks_ref[chunk, tile] = jnp.concatenate([wet, bed, pad], axis=0)
        for copy in sends(chunk):
            copy.start()
        return 0

    lax.fori_loop(0, chunks, step, 0)
    for chunk in range(chunks):
        for copy in sends(chunk):
            copy.wait()


def floc_body(xs, place_ref, rate_ref, *refs):
    hbm, rest = refs[:6], refs[-10:]
    floc_hbm, held = rest[0], rest[1:7]
    out_ref, in_sems, out_sems = rest[7:]
    chunks, depth, _, classes, width = held[0].shape
    for chunk in range(chunks):
        for copy in chunk_copies(xs, place_ref, hbm, held, in_sems, chunk):
            copy.start()

    def send(chunk):
        to = floc_hbm.at[:, pl.ds(xs[0], len(xs)), :, pl.ds(chunk * width, width)]
        return pltpu.make_async_copy(out_ref.at[chunk], to, out_sems.at[chunk])

    def step(chunk, _):
        for copy in chunk_copies(xs, place_ref, hbm, held, in_sems, chunk):
            copy.wait()

        def start(tile, n):
            return held[5][chunk, tile, n * classes : (n + 1) * classes, :]

        def emit(tile, n, k, above, carry):
            cols = slice(tile * LANES, (tile + 1) * LANES)
            out_ref[chunk, k, n, :, cols] = jnp.where(above, carry, 0.0).astype(BF16)

        settle_block(xs, place_ref[0] * depth, chunk, *held[:3], rate_ref, *held[3:5], start, emit)
        send(chunk).start()
        return 0

    lax.fori_loop(0, chunks, step, 0)
    for chunk in range(chunks):
        send(chunk).wait()


def settle_call(body, xs, name, place, operands, into, out_shape, extra_scratch, tiles):
    conc, change, flow, rate, wet, bed, *inflow = operands
    depth, rows, classes, width = conc.shape
    cols = tiles * LANES
    chunks = width // cols
    scratch = [
        pltpu.VMEM((chunks, depth, len(xs), classes, cols), BF16),
        pltpu.VMEM((chunks, depth, len(xs), classes, cols), F32),
        pltpu.VMEM((chunks, tiles) + flow.shape[1:], F32),
        pltpu.VMEM((chunks, rows, cols), jnp.int32),
        pltpu.VMEM((chunks, rows, cols), jnp.int32),
    ]
    scratch += [pltpu.VMEM((chunks, tiles) + part.shape[1:], F32) for part in inflow]
    scratch += extra_scratch(chunks, cols)
    args = [place, rate, conc, change, flow, wet, bed, *inflow, *into]
    in_specs = [pl.BlockSpec(memory_space=pltpu.SMEM), pl.BlockSpec(memory_space=pltpu.VMEM)]
    in_specs += [pl.BlockSpec(memory_space=pl.ANY)] * (len(args) - 2)
    some = depth * len(xs) * classes * width
    return pl.pallas_call(
        partial(body, xs),
        out_shape=out_shape,
        in_specs=in_specs,
        out_specs=jax.tree.map(lambda _: pl.BlockSpec(memory_space=pl.ANY), out_shape),
        scratch_shapes=scratch,
        input_output_aliases={len(args) - 1: 0} if into else {},
        compiler_params=pltpu.CompilerParams(vmem_limit_bytes=VMEM_BYTES),
        cost_estimate=pl.CostEstimate(flops=12 * some, bytes_accessed=8 * some, transcendentals=some),
        name=name,
    )(*args)


def through_body(place_ref, flow_ref, marks_ref, rate_ref, through_ref):
    levels = flow_ref.shape[1]
    sources = marks_ref.shape[0]
    rows = through_ref.shape[0] // sources
    shape = through_ref.shape[1:]
    for source in range(sources):
        for x in range(rows):
            row = source * rows + x
            speed = marks_ref[source, x : x + 1, :] * rate_ref[...]
            bed = jnp.broadcast_to(marks_ref[source, rows + x : rows + x + 1, :], shape)
            through = jnp.ones(shape, F32)
            for k in range(levels):
                thick = flow_ref[0, k, row : row + 1, :]
                keep = speed * reciprocal(thick + speed)
                through = jnp.where(bed >= float(levels + k), through * keep, through)
            through_ref[row] = through


def near_body(place_ref, through_ref, own_ref, other_ref, near_ref):
    sources = own_ref.shape[0]
    classes = through_ref.shape[1]
    rows = through_ref.shape[0] // sources
    is_upper = place_ref[0] == 0
    for source in range(sources):
        for x in range(rows):
            part = slice(x * classes, (x + 1) * classes)
            own = own_ref[source, part, :]
            other = other_ref[source, part, :]
            upper = jnp.where(is_upper, own, other)
            lower = jnp.where(is_upper, other, own)
            near_ref[source * rows + x] = through_ref[source * rows + x] * upper + lower


def local(concentration, flow_planes, agg_kernel, settle_rate, wet_mask, bed_level):
    depth, rows, classes, width = concentration.shape
    planes, levels, tall, _ = flow_planes.shape
    groups, spread = lax.axis_size("lev"), lax.axis_size("horiz")
    lev, horiz = lax.axis_index("lev"), lax.axis_index("horiz")
    share = spread // groups
    place = jnp.stack([lev, horiz // share]).astype(jnp.int32)
    rate = jnp.broadcast_to(settle_rate[:, None], (classes, LANES))

    slots = flow_planes.reshape(planes, groups, depth, share, rows, LANES).transpose(1, 3, 0, 2, 4, 5)
    slots = jnp.broadcast_to(slots[:, None], (groups, groups) + slots.shape[1:])
    slots = slots.reshape(groups * spread, planes * depth * rows, LANES)
    flow = lax.all_to_all(slots, ("lev", "horiz"), split_axis=0, concat_axis=0, tiled=True)

    change = change_of(pair_weights(agg_kernel, classes), concentration)

    operands = (concentration, change, flow, rate, wet_mask, bed_level)
    tiles = 8
    held = rows * classes
    marked = held + 8 * pl.cdiv(2 * rows, 8)
    slab = jax.ShapeDtypeStruct((spread, classes, LANES), F32)
    flux_early, flux_late, sent = settle_call(
        flux_body,
        (0, 1),
        "flux",
        place,
        operands,
        [],
        (slab, slab, jax.ShapeDtypeStruct((spread, marked, LANES), F32)),
        lambda chunks, cols: [
            pltpu.VMEM((chunks, tiles, held, LANES), F32),
            pltpu.VMEM((chunks, tiles, marked - held, LANES), F32),
            pltpu.SemaphoreType.DMA((5, chunks)),
            pltpu.SemaphoreType.DMA((4, chunks)),
        ],
        tiles,
    )

    def beside(at):
        return at ^ BESIDE

    both = ("lev", "horiz")
    crossing = [(at, spread + beside(at)) for at in range(spread)]
    returning = [(spread + at, beside(at)) for at in range(spread)]
    swapping = [(spread + at, spread + beside(at)) for at in range(spread)]
    crossed = lax.ppermute(flux_early, both, crossing)
    spread_out = lax.all_to_all(sent, "horiz", split_axis=0, concat_axis=0, tiled=True)
    crossed, flux_late = lax.optimization_barrier((crossed, flux_late))
    inflow_early = lax.ppermute(crossed, both, swapping)
    inflow_late = lax.ppermute(flux_late, "lev", [(0, 1)])
    away = lax.dynamic_slice(spread_out, ((1 - lev) * share, 0, 0), (share, held, LANES))
    other = lax.ppermute(away, both, crossing + returning)

    floc = []
    for x, inflow in ((0, inflow_early), (1, inflow_late)):
        floc = settle_call(
            floc_body,
            (x,),
            "floc",
            place,
            operands + (inflow,),
            floc,
            [jax.ShapeDtypeStruct(concentration.shape, BF16)],
            lambda chunks, cols: [
                pltpu.VMEM((chunks, depth, 1, classes, cols), BF16),
                pltpu.SemaphoreType.DMA((6, chunks)),
                pltpu.SemaphoreType.DMA((chunks,)),
            ],
            tiles,
        )
    floc = floc[0]

    near_shape = (tall, classes, LANES)
    some = 8
    steps = share // some
    near_block = pl.BlockSpec((some * rows, classes, LANES), lambda i, place: (i, 0, 0))
    through = pl.pallas_call(
        through_body,
        out_shape=jax.ShapeDtypeStruct(near_shape, F32),
        grid_spec=pltpu.PrefetchScalarGridSpec(
            num_scalar_prefetch=1,
            grid=(steps,),
            in_specs=[
                pl.BlockSpec((1, depth, some * rows, LANES), lambda i, place: (1, 1, i, 0)),
                pl.BlockSpec(
                    (some, marked - held, LANES),
                    lambda i, place: (place[0] * steps + i, held // (marked - held), 0),
                ),
                pl.BlockSpec(rate.shape, lambda i, place: (0, 0)),
            ],
            out_specs=near_block,
        ),
        cost_estimate=pl.CostEstimate(
            flops=8 * depth * tall * classes * LANES,
            bytes_accessed=8 * tall * classes * LANES,
            transcendentals=depth * tall * classes * LANES,
        ),
        name="through",
    )(place, flow_planes, spread_out, rate)
    near_bed = pl.pallas_call(
        near_body,
        out_shape=jax.ShapeDtypeStruct(near_shape, F32),
        grid_spec=pltpu.PrefetchScalarGridSpec(
            num_scalar_prefetch=1,
            grid=(steps,),
            in_specs=[
                near_block,
                pl.BlockSpec((some, held, LANES), lambda i, place: (place[0] * steps + i, 0, 0)),
                pl.BlockSpec((some, held, LANES), lambda i, place: (i, 0, 0)),
            ],
            out_specs=near_block,
        ),
        cost_estimate=pl.CostEstimate(
            flops=2 * tall * classes * LANES,
            bytes_accessed=16 * tall * classes * LANES,
            transcendentals=0,
        ),
        name="near",
    )(place, through, spread_out, other)
    return (floc, near_bed)


def solution(mesh):
    in_specs = (
        P("lev", "horiz", None, None),
        P(None, None, "lev", "horiz"),
        P(),
        P(),
        P("horiz", None),
        P("horiz", None),
    )
    out_specs = (P("lev", "horiz", None, None), P("lev", None, "horiz"))
    return jax.shard_map(local, mesh=mesh, in_specs=in_specs, out_specs=out_specs, check_vma=False)
```

```python
from functools import partial

import jax
import jax.numpy as jnp
import numpy as np
from jax import lax
from jax.experimental import pallas as pl
from jax.experimental.pallas import tpu as pltpu
from jax.sharding import PartitionSpec as P

LANES = 128
BESIDE = 8
F32 = jnp.float32
BF16 = jnp.bfloat16
VMEM_BYTES = 56 << 20
SETTLE_BYTES = 50 << 20
NEAR_BYTES = 16 << 20


def pair_order(classes):
    half = classes // 2
    order = [(one, half + two) for one in range(half) for two in range(half)]
    for base in (0, half):
        for shift in range(half // 2):
            order += [(base + one, base + (one + shift) % half) for one in range(half)]
    for base in (0, half):
        order += [(base + one, base + one + half // 2) for one in range(half // 2)]
    return order


def pair_weights(agg_kernel, classes):
    order = pair_order(classes)
    chosen = np.zeros((classes * classes, len(order)), np.float32)
    for place, (one, two) in enumerate(order):
        chosen[one * classes + two, place] = 1.0
        chosen[two * classes + one, place] = 1.0
    rows = lax.dot_general(
        agg_kernel, jnp.asarray(chosen, BF16), (((0,), (0,)), ((), ())), preferred_element_type=F32
    )
    high = lax.reduce_precision(rows, 8, 7)
    return jnp.concatenate([high, rows - high], axis=0).astype(BF16)


def pair_rows(conc):
    half = conc.shape[0] // 2
    quarter = half // 2
    halves = [conc[:half], conc[half:]]
    wide = [part.astype(F32) for part in halves]
    pairs = [
        halves[1] * jnp.broadcast_to(conc[one : one + 1], halves[1].shape) for one in range(half)
    ]
    for part, whole in zip(halves, wide):
        pairs.append(part * part)
        for shift in range(1, quarter):
            pairs.append(part * pltpu.roll(whole, half - shift, axis=0).astype(BF16))
    last = [whole[:quarter] * whole[quarter:] for whole in wide]
    pairs.append(jnp.concatenate(last, axis=0).astype(BF16))
    return jnp.concatenate(pairs, axis=0)


def change_body(step, weight_ref, conc_ref, change_ref):
    classes, width = conc_ref.shape[2:]
    cols = change_ref.shape[-1]
    for start in range(0, width, step):
        both = lax.dot_general(
            weight_ref[...],
            pair_rows(conc_ref[0, 0, :, start : start + step]),
            (((1,), (0,)), ((), ())),
            preferred_element_type=F32,
        )
        change = both[:classes] + both[classes:]
        for part in range(step // cols):
            change_ref[start // cols + part, 0, 0] = change[:, part * cols : (part + 1) * cols]


def change_of(weights, conc, cols):
    depth, rows, classes, width = conc.shape
    chunks = width // cols
    return pl.pallas_call(
        partial(change_body, 2 * cols),
        out_shape=jax.ShapeDtypeStruct((chunks, depth, rows, classes, cols), F32),
        grid=(depth, rows),
        in_specs=[
            pl.BlockSpec(weights.shape, lambda k, x: (0, 0)),
            pl.BlockSpec((1, 1, classes, width), lambda k, x: (k, x, 0, 0)),
        ],
        out_specs=pl.BlockSpec((chunks, 1, 1, classes, cols), lambda k, x: (0, k, x, 0, 0)),
        compiler_params=pltpu.CompilerParams(vmem_limit_bytes=VMEM_BYTES),
        cost_estimate=pl.CostEstimate(
            flops=2 * weights.size * depth * rows * width,
            bytes_accessed=6 * conc.size,
            transcendentals=0,
        ),
        name="change",
    )(weights, conc)


def reciprocal(x):
    return pl.reciprocal(x, approx=True)


def settle_block(xs, first_level, chunk, conc_ref, change_ref, flow_ref, rate_ref, wet_ref, bed_ref, start, emit):
    _, depth, _, classes, width = conc_ref.shape
    rows = wet_ref.shape[1]
    for tile in range(width // LANES):
        cols = slice(tile * LANES, (tile + 1) * LANES)
        for n, x in enumerate(xs):
            wet = wet_ref[chunk, x : x + 1, cols].astype(F32)
            bed = jnp.broadcast_to(bed_ref[chunk, x : x + 1, cols] - first_level, (classes, LANES))
            speed = wet * jnp.broadcast_to(rate_ref[...], (classes, LANES))
            carry = start(tile, n)
            for k in range(depth):
                shear = flow_ref[chunk, tile, k * rows + x : k * rows + x + 1, :]
                at = (depth + k) * rows + x
                thick = flow_ref[chunk, tile, at : at + 1, :]
                change = change_ref[chunk, k, n, :, cols]
                aggregated = conc_ref[chunk, k, n, :, cols].astype(F32) + (wet * shear) * change
                settled = (speed * carry + thick * aggregated) * reciprocal(thick + speed)
                above = k <= bed
                carry = jnp.where(above, settled, carry)
                emit(tile, n, k, above, carry)


def chunk_copies(xs, place_ref, hbm, held, sems, chunk):
    chunks = held[0].shape[0]
    width = held[0].shape[-1]
    tiles = held[2].shape[1]
    cols = pl.ds(chunk * width, width)
    some = pl.ds(xs[0], len(xs))
    parts = [
        hbm[0].at[:, some, :, cols],
        hbm[1].at[chunk, :, some],
        hbm[2].at[pl.ds(place_ref[1] * (chunks * tiles) + chunk * tiles, tiles)],
        hbm[3].at[:, cols],
        hbm[4].at[:, cols],
    ]
    if len(held) > 5:
        parts.append(hbm[5].at[pl.ds(chunk * tiles, tiles)])
    return [
        pltpu.make_async_copy(part, held[at].at[chunk], sems.at[at, chunk])
        for at, part in enumerate(parts)
    ]


def flux_body(xs, place_ref, rate_ref, *refs):
    hbm, flux_hbm, sent_hbm, held = refs[:5], refs[5:7], refs[7], refs[8:13]
    value_ref, marks_ref, in_sems, out_sems = refs[13:]
    chunks, depth, rows, classes, _ = held[0].shape
    tiles = held[2].shape[1]
    for chunk in range(chunks):
        for copy in chunk_copies(xs, place_ref, hbm, held, in_sems, chunk):
            copy.start()
    zero = jnp.zeros((classes, LANES), F32)
    turned = jnp.where(place_ref[0] == place_ref[1], 0, 1)

    def sends(chunk):
        here = pl.ds(chunk * tiles, tiles)
        to = pl.ds(jnp.bitwise_xor(chunk, turned) * tiles, tiles)
        top = rows * classes
        copies = [
            pltpu.make_async_copy(
                value_ref.at[chunk, :, pl.ds(n * classes, classes)], part.at[here], out_sems.at[n, chunk]
            )
            for n, part in enumerate(flux_hbm)
        ]
        copies.append(
            pltpu.make_async_copy(
                value_ref.at[chunk], sent_hbm.at[to, pl.ds(0, top)], out_sems.at[2, chunk]
            )
        )
        copies.append(
            pltpu.make_async_copy(
                marks_ref.at[chunk], sent_hbm.at[to, pl.ds(top, marks_ref.shape[2])], out_sems.at[3, chunk]
            )
        )
        return copies

    def step(chunk, _):
        for copy in chunk_copies(xs, place_ref, hbm, held, in_sems, chunk):
            copy.wait()

        def emit(tile, n, k, above, carry):
            if k == depth - 1:
                value_ref[chunk, tile, n * classes : (n + 1) * classes, :] = carry

        settle_block(
            xs, place_ref[0] * depth, chunk, *held[:3], rate_ref, *held[3:], lambda tile, n: zero, emit
        )
        for tile in range(tiles):
            cols = slice(tile * LANES, (tile + 1) * LANES)
            wet = held[3][chunk, :, cols].astype(F32)
            bed = held[4][chunk, :, cols].astype(F32)
            pad = jnp.zeros((marks_ref.shape[2] - 2 * rows, LANES), F32)
            marks_ref[chunk, tile] = jnp.concatenate([wet, bed, pad], axis=0)
        for copy in sends(chunk):
            copy.start()
        return 0

    lax.fori_loop(0, chunks, step, 0)
    for chunk in range(chunks):
        for copy in sends(chunk):
            copy.wait()


def floc_body(xs, place_ref, rate_ref, *refs):
    hbm, rest = refs[:6], refs[-10:]
    floc_hbm, held = rest[0], rest[1:7]
    out_ref, in_sems, out_sems = rest[7:]
    chunks, depth, _, classes, width = held[0].shape
    for chunk in range(chunks):
        for copy in chunk_copies(xs, place_ref, hbm, held, in_sems, chunk):
            copy.start()

    def send(chunk):
        to = floc_hbm.at[:, pl.ds(xs[0], len(xs)), :, pl.ds(chunk * width, width)]
        return pltpu.make_async_copy(out_ref.at[chunk], to, out_sems.at[chunk])

    def step(chunk, _):
        for copy in chunk_copies(xs, place_ref, hbm, held, in_sems, chunk):
            copy.wait()

        def start(tile, n):
            return held[5][chunk, tile, n * classes : (n + 1) * classes, :]

        def emit(tile, n, k, above, carry):
            cols = slice(tile * LANES, (tile + 1) * LANES)
            out_ref[chunk, k, n, :, cols] = jnp.where(above, carry, 0.0).astype(BF16)

        settle_block(xs, place_ref[0] * depth, chunk, *held[:3], rate_ref, *held[3:5], start, emit)
        send(chunk).start()
        return 0

    lax.fori_loop(0, chunks, step, 0)
    for chunk in range(chunks):
        send(chunk).wait()


def settle_call(body, xs, name, place, operands, into, out_shape, extra_scratch, tiles):
    conc, change, flow, rate, wet, bed, *inflow = operands
    depth, rows, classes, width = conc.shape
    cols = tiles * LANES
    chunks = width // cols
    scratch = [
        pltpu.VMEM((chunks, depth, len(xs), classes, cols), BF16),
        pltpu.VMEM((chunks, depth, len(xs), classes, cols), F32),
        pltpu.VMEM((chunks, tiles) + flow.shape[1:], F32),
        pltpu.VMEM((chunks, rows, cols), jnp.int32),
        pltpu.VMEM((chunks, rows, cols), jnp.int32),
    ]
    scratch += [pltpu.VMEM((chunks, tiles) + part.shape[1:], F32) for part in inflow]
    scratch += extra_scratch(chunks, cols)
    args = [place, rate, conc, change, flow, wet, bed, *inflow, *into]
    in_specs = [pl.BlockSpec(memory_space=pltpu.SMEM), pl.BlockSpec(memory_space=pltpu.VMEM)]
    in_specs += [pl.BlockSpec(memory_space=pl.ANY)] * (len(args) - 2)
    some = depth * len(xs) * classes * width
    return pl.pallas_call(
        partial(body, xs),
        out_shape=out_shape,
        in_specs=in_specs,
        out_specs=jax.tree.map(lambda _: pl.BlockSpec(memory_space=pl.ANY), out_shape),
        scratch_shapes=scratch,
        input_output_aliases={len(args) - 1: 0} if into else {},
        compiler_params=pltpu.CompilerParams(vmem_limit_bytes=SETTLE_BYTES),
        cost_estimate=pl.CostEstimate(flops=12 * some, bytes_accessed=8 * some, transcendentals=some),
        name=name,
    )(*args)


def through_body(place_ref, flow_ref, marks_ref, rate_ref, through_ref):
    levels = flow_ref.shape[1]
    sources = marks_ref.shape[0]
    rows = through_ref.shape[0] // sources
    shape = through_ref.shape[1:]
    for source in range(sources):
        for x in range(rows):
            row = source * rows + x
            speed = marks_ref[source, x : x + 1, :] * jnp.broadcast_to(rate_ref[...], shape)
            bed = jnp.broadcast_to(marks_ref[source, rows + x : rows + x + 1, :], shape)
            through = jnp.ones(shape, F32)
            for k in range(levels):
                thick = flow_ref[0, k, row : row + 1, :]
                keep = speed * reciprocal(thick + speed)
                through = jnp.where(bed >= float(levels + k), through * keep, through)
            through_ref[row] = through


def near_body(place_ref, through_ref, own_ref, other_ref, near_ref):
    sources = own_ref.shape[0]
    classes = through_ref.shape[1]
    rows = through_ref.shape[0] // sources
    is_upper = place_ref[0] == 0
    for source in range(sources):
        for x in range(rows):
            part = slice(x * classes, (x + 1) * classes)
            own = own_ref[source, part, :]
            other = other_ref[source, part, :]
            upper = jnp.where(is_upper, own, other)
            lower = jnp.where(is_upper, other, own)
            near_ref[source * rows + x] = through_ref[source * rows + x] * upper + lower


def local(concentration, flow_planes, agg_kernel, settle_rate, wet_mask, bed_level):
    depth, rows, classes, width = concentration.shape
    planes, levels, tall, _ = flow_planes.shape
    groups, spread = lax.axis_size("lev"), lax.axis_size("horiz")
    lev, horiz = lax.axis_index("lev"), lax.axis_index("horiz")
    share = spread // groups
    place = jnp.stack([lev, horiz // share]).astype(jnp.int32)
    rate = settle_rate[:, None]

    slots = flow_planes.reshape(planes, groups, depth, share, rows, LANES).transpose(1, 3, 0, 2, 4, 5)
    slots = jnp.broadcast_to(slots[:, None], (groups, groups) + slots.shape[1:])
    slots = slots.reshape(groups * spread, planes * depth * rows, LANES)
    flow = lax.all_to_all(slots, ("lev", "horiz"), split_axis=0, concat_axis=0, tiled=True)

    tiles = 8
    change = change_of(pair_weights(agg_kernel, classes), concentration, tiles * LANES)

    operands = (concentration, change, flow, rate, wet_mask, bed_level)
    held = rows * classes
    marked = held + 8 * pl.cdiv(2 * rows, 8)
    slab = jax.ShapeDtypeStruct((spread, classes, LANES), F32)
    flux_early, flux_late, sent = settle_call(
        flux_body,
        (0, 1),
        "flux",
        place,
        operands,
        [],
        (slab, slab, jax.ShapeDtypeStruct((spread, marked, LANES), F32)),
        lambda chunks, cols: [
            pltpu.VMEM((chunks, tiles, held, LANES), F32),
            pltpu.VMEM((chunks, tiles, marked - held, LANES), F32),
            pltpu.SemaphoreType.DMA((5, chunks)),
            pltpu.SemaphoreType.DMA((4, chunks)),
        ],
        tiles,
    )

    def beside(at):
        return at ^ BESIDE

    both = ("lev", "horiz")
    crossing = [(at, spread + beside(at)) for at in range(spread)]
    returning = [(spread + at, beside(at)) for at in range(spread)]
    swapping = [(spread + at, spread + beside(at)) for at in range(spread)]
    crossed = lax.ppermute(flux_early, both, crossing)
    spread_out = lax.all_to_all(sent, "horiz", split_axis=0, concat_axis=0, tiled=True)
    crossed, flux_late = lax.optimization_barrier((crossed, flux_late))
    inflow_early = lax.ppermute(crossed, both, swapping)
    inflow_late = lax.ppermute(flux_late, "lev", [(0, 1)])
    away = lax.dynamic_slice(spread_out, ((1 - lev) * share, 0, 0), (share, held, LANES))
    other = lax.ppermute(away, both, crossing + returning)

    floc = []
    for x, inflow in ((0, inflow_early), (1, inflow_late)):
        floc = settle_call(
            floc_body,
            (x,),
            "floc",
            place,
            operands + (inflow,),
            floc,
            [jax.ShapeDtypeStruct(concentration.shape, BF16)],
            lambda chunks, cols: [
                pltpu.VMEM((chunks, depth, 1, classes, cols), BF16),
                pltpu.SemaphoreType.DMA((6, chunks)),
                pltpu.SemaphoreType.DMA((chunks,)),
            ],
            tiles,
        )
    floc = floc[0]

    near_shape = (tall, classes, LANES)
    some = 16
    steps = share // some
    near_block = pl.BlockSpec((some * rows, classes, LANES), lambda i, place: (i, 0, 0))
    through = pl.pallas_call(
        through_body,
        out_shape=jax.ShapeDtypeStruct(near_shape, F32),
        grid_spec=pltpu.PrefetchScalarGridSpec(
            num_scalar_prefetch=1,
            grid=(steps,),
            in_specs=[
                pl.BlockSpec((1, depth, some * rows, LANES), lambda i, place: (1, 1, i, 0)),
                pl.BlockSpec(
                    (some, marked - held, LANES),
                    lambda i, place: (place[0] * steps + i, held // (marked - held), 0),
                ),
                pl.BlockSpec(rate.shape, lambda i, place: (0, 0)),
            ],
            out_specs=near_block,
        ),
        compiler_params=pltpu.CompilerParams(vmem_limit_bytes=NEAR_BYTES),
        cost_estimate=pl.CostEstimate(
            flops=8 * depth * tall * classes * LANES,
            bytes_accessed=8 * tall * classes * LANES,
            transcendentals=depth * tall * classes * LANES,
        ),
        name="through",
    )(place, flow_planes, spread_out, rate)
    near_bed = pl.pallas_call(
        near_body,
        out_shape=jax.ShapeDtypeStruct(near_shape, F32),
        grid_spec=pltpu.PrefetchScalarGridSpec(
            num_scalar_prefetch=1,
            grid=(steps,),
            in_specs=[
                near_block,
                pl.BlockSpec((some, held, LANES), lambda i, place: (place[0] * steps + i, 0, 0)),
                pl.BlockSpec((some, held, LANES), lambda i, place: (i, 0, 0)),
            ],
            out_specs=near_block,
        ),
        compiler_params=pltpu.CompilerParams(vmem_limit_bytes=NEAR_BYTES),
        cost_estimate=pl.CostEstimate(
            flops=2 * tall * classes * LANES,
            bytes_accessed=16 * tall * classes * LANES,
            transcendentals=0,
        ),
        name="near",
    )(place, through, spread_out, other)
    return (floc, near_bed)


def solution(mesh):
    in_specs = (
        P("lev", "horiz", None, None),
        P(None, None, "lev", "horiz"),
        P(),
        P(),
        P("horiz", None),
        P("horiz", None),
    )
    out_specs = (P("lev", "horiz", None, None), P("lev", None, "horiz"))
    return jax.shard_map(local, mesh=mesh, in_specs=in_specs, out_specs=out_specs, check_vma=False)
```

```python
from functools import partial

import jax
import jax.numpy as jnp
import numpy as np
from jax import lax
from jax.experimental import pallas as pl
from jax.experimental.pallas import tpu as pltpu
from jax.sharding import PartitionSpec as P

LANES = 128
BESIDE = 8
F32 = jnp.float32
BF16 = jnp.bfloat16
VMEM_BYTES = 56 << 20
SETTLE_BYTES = 50 << 20
NEAR_BYTES = 16 << 20


def pair_order(classes):
    half = classes // 2
    order = [(one, half + two) for one in range(half) for two in range(half)]
    for base in (0, half):
        for shift in range(half // 2):
            order += [(base + one, base + (one + shift) % half) for one in range(half)]
    for base in (0, half):
        order += [(base + one, base + one + half // 2) for one in range(half // 2)]
    return order


def pair_weights(agg_kernel, classes):
    order = pair_order(classes)
    chosen = np.zeros((classes * classes, len(order)), np.float32)
    for place, (one, two) in enumerate(order):
        chosen[one * classes + two, place] = 1.0
        chosen[two * classes + one, place] = 1.0
    rows = lax.dot_general(
        agg_kernel, jnp.asarray(chosen, BF16), (((0,), (0,)), ((), ())), preferred_element_type=F32
    )
    high = lax.reduce_precision(rows, 8, 7)
    return jnp.concatenate([high, rows - high], axis=0).astype(BF16)


def pair_rows(conc):
    half = conc.shape[0] // 2
    quarter = half // 2
    halves = [conc[:half], conc[half:]]
    wide = [part.astype(F32) for part in halves]
    pairs = [
        halves[1] * jnp.broadcast_to(conc[one : one + 1], halves[1].shape) for one in range(half)
    ]
    for part, whole in zip(halves, wide):
        pairs.append(part * part)
        for shift in range(1, quarter):
            pairs.append(part * pltpu.roll(whole, half - shift, axis=0).astype(BF16))
    last = [whole[:quarter] * whole[quarter:] for whole in wide]
    pairs.append(jnp.concatenate(last, axis=0).astype(BF16))
    return jnp.concatenate(pairs, axis=0)


def change_body(step, weight_ref, conc_ref, change_ref):
    classes, width = conc_ref.shape[2:]
    cols = change_ref.shape[-1]
    for start in range(0, width, step):
        both = lax.dot_general(
            weight_ref[...],
            pair_rows(conc_ref[0, 0, :, start : start + step]),
            (((1,), (0,)), ((), ())),
            preferred_element_type=F32,
        )
        change = both[:classes] + both[classes:]
        for part in range(step // cols):
            change_ref[start // cols + part, 0, 0] = change[:, part * cols : (part + 1) * cols]


def change_of(weights, conc, cols):
    depth, rows, classes, width = conc.shape
    chunks = width // cols
    return pl.pallas_call(
        partial(change_body, 2 * cols),
        out_shape=jax.ShapeDtypeStruct((chunks, depth, rows, classes, cols), F32),
        grid=(depth, rows),
        in_specs=[
            pl.BlockSpec(weights.shape, lambda k, x: (0, 0)),
            pl.BlockSpec((1, 1, classes, width), lambda k, x: (k, x, 0, 0)),
        ],
        out_specs=pl.BlockSpec((chunks, 1, 1, classes, cols), lambda k, x: (0, k, x, 0, 0)),
        compiler_params=pltpu.CompilerParams(vmem_limit_bytes=VMEM_BYTES),
        cost_estimate=pl.CostEstimate(
            flops=2 * weights.size * depth * rows * width,
            bytes_accessed=6 * conc.size,
            transcendentals=0,
        ),
        name="change",
    )(weights, conc)


def reciprocal(x):
    return pl.reciprocal(x, approx=True)


def settle_block(xs, first_level, chunk, conc_ref, change_ref, flow_ref, rate_ref, wet_ref, bed_ref, start, emit):
    _, depth, _, classes, width = conc_ref.shape
    rows = wet_ref.shape[1]
    for tile in range(width // LANES):
        cols = slice(tile * LANES, (tile + 1) * LANES)
        for n, x in enumerate(xs):
            wet = wet_ref[chunk, x : x + 1, cols].astype(F32)
            bed = jnp.broadcast_to(bed_ref[chunk, x : x + 1, cols] - first_level, (classes, LANES))
            speed = wet * jnp.broadcast_to(rate_ref[...], (classes, LANES))
            carry = start(tile, n)
            for k in range(depth):
                shear = flow_ref[chunk, tile, k * rows + x : k * rows + x + 1, :]
                at = (depth + k) * rows + x
                thick = flow_ref[chunk, tile, at : at + 1, :]
                change = change_ref[chunk, k, n, :, cols]
                aggregated = conc_ref[chunk, k, n, :, cols].astype(F32) + (wet * shear) * change
                settled = (speed * carry + thick * aggregated) * reciprocal(thick + speed)
                above = k <= bed
                carry = jnp.where(above, settled, carry)
                emit(tile, n, k, above, carry)


def chunk_copies(xs, place_ref, hbm, held, sems, chunk):
    chunks = held[0].shape[0]
    width = held[0].shape[-1]
    tiles = held[2].shape[1]
    cols = pl.ds(chunk * width, width)
    some = pl.ds(xs[0], len(xs))
    parts = [
        hbm[0].at[:, some, :, cols],
        hbm[1].at[chunk, :, some],
        hbm[2].at[pl.ds(place_ref[1] * (chunks * tiles) + chunk * tiles, tiles)],
        hbm[3].at[:, cols],
        hbm[4].at[:, cols],
    ]
    if len(hbm) > 5:
        part, at = hbm[5], 0
        if isinstance(chunk, int):
            at = chunk * tiles
            for part in hbm[5:]:
                if at < part.shape[0]:
                    break
                at -= part.shape[0]
        parts.append(part.at[pl.ds(at, tiles)])
    return [
        pltpu.make_async_copy(part, held[at].at[chunk], sems.at[at, chunk])
        for at, part in enumerate(parts)
    ]


def flux_body(xs, place_ref, rate_ref, *refs):
    hbm, early_hbm, late_hbm, sent_hbm, held = refs[:5], refs[5], refs[6:8], refs[8], refs[9:14]
    value_ref, marks_ref, in_sems, out_sems = refs[14:]
    chunks, depth, rows, classes, _ = held[0].shape
    tiles = held[2].shape[1]
    for chunk in range(chunks):
        for copy in chunk_copies(xs, place_ref, hbm, held, in_sems, chunk):
            copy.start()
    zero = jnp.zeros((classes, LANES), F32)
    turned = jnp.where(place_ref[0] == place_ref[1], 0, 1)

    cut = late_hbm[0].shape[0] // tiles
    spans = ((0, cut), (cut, chunks))

    def sends(part, chunk):
        here = pl.ds(chunk * tiles, tiles)
        there = pl.ds((chunk - spans[part][0]) * tiles, tiles)
        to = pl.ds(jnp.bitwise_xor(chunk, turned) * tiles, tiles)
        top = rows * classes
        first, second = pl.ds(0, classes), pl.ds(classes, classes)
        return [
            pltpu.make_async_copy(value_ref.at[chunk, :, first], early_hbm.at[here], out_sems.at[0, chunk]),
            pltpu.make_async_copy(
                value_ref.at[chunk, :, second], late_hbm[part].at[there], out_sems.at[1, chunk]
            ),
            pltpu.make_async_copy(
                value_ref.at[chunk], sent_hbm.at[to, pl.ds(0, top)], out_sems.at[2, chunk]
            ),
            pltpu.make_async_copy(
                marks_ref.at[chunk], sent_hbm.at[to, pl.ds(top, marks_ref.shape[2])], out_sems.at[3, chunk]
            ),
        ]

    def step(part, chunk, _):
        for copy in chunk_copies(xs, place_ref, hbm, held, in_sems, chunk):
            copy.wait()

        def emit(tile, n, k, above, carry):
            if k == depth - 1:
                value_ref[chunk, tile, n * classes : (n + 1) * classes, :] = carry

        settle_block(
            xs, place_ref[0] * depth, chunk, *held[:3], rate_ref, *held[3:], lambda tile, n: zero, emit
        )
        for tile in range(tiles):
            cols = slice(tile * LANES, (tile + 1) * LANES)
            wet = held[3][chunk, :, cols].astype(F32)
            bed = held[4][chunk, :, cols].astype(F32)
            pad = jnp.zeros((marks_ref.shape[2] - 2 * rows, LANES), F32)
            marks_ref[chunk, tile] = jnp.concatenate([wet, bed, pad], axis=0)
        for copy in sends(part, chunk):
            copy.start()
        return 0

    for part, span in enumerate(spans):
        lax.fori_loop(*span, partial(step, part), 0)
    for part, span in enumerate(spans):
        for chunk in range(*span):
            for copy in sends(part, chunk):
                copy.wait()


def floc_body(parts, xs, place_ref, rate_ref, *refs):
    hbm, rest = refs[: 5 + parts], refs[-10:]
    floc_hbm, held = rest[0], rest[1:7]
    out_ref, in_sems, out_sems = rest[7:]
    chunks, depth, _, classes, width = held[0].shape
    for chunk in range(chunks):
        for copy in chunk_copies(xs, place_ref, hbm, held, in_sems, chunk):
            copy.start()

    def send(chunk):
        to = floc_hbm.at[:, pl.ds(xs[0], len(xs)), :, pl.ds(chunk * width, width)]
        return pltpu.make_async_copy(out_ref.at[chunk], to, out_sems.at[chunk])

    def step(chunk, _):
        for copy in chunk_copies(xs, place_ref, hbm, held, in_sems, chunk):
            copy.wait()

        def start(tile, n):
            return held[5][chunk, tile, n * classes : (n + 1) * classes, :]

        def emit(tile, n, k, above, carry):
            cols = slice(tile * LANES, (tile + 1) * LANES)
            out_ref[chunk, k, n, :, cols] = jnp.where(above, carry, 0.0).astype(BF16)

        settle_block(xs, place_ref[0] * depth, chunk, *held[:3], rate_ref, *held[3:5], start, emit)
        send(chunk).start()
        return 0

    lax.fori_loop(0, chunks, step, 0)
    for chunk in range(chunks):
        send(chunk).wait()


def settle_call(body, xs, name, place, operands, into, out_shape, extra_scratch, tiles):
    conc, change, flow, rate, wet, bed, *inflow = operands
    depth, rows, classes, width = conc.shape
    cols = tiles * LANES
    chunks = width // cols
    scratch = [
        pltpu.VMEM((chunks, depth, len(xs), classes, cols), BF16),
        pltpu.VMEM((chunks, depth, len(xs), classes, cols), F32),
        pltpu.VMEM((chunks, tiles) + flow.shape[1:], F32),
        pltpu.VMEM((chunks, rows, cols), jnp.int32),
        pltpu.VMEM((chunks, rows, cols), jnp.int32),
    ]
    if inflow:
        scratch.append(pltpu.VMEM((chunks, tiles) + inflow[0].shape[1:], F32))
    scratch += extra_scratch(chunks, cols)
    args = [place, rate, conc, change, flow, wet, bed, *inflow, *into]
    in_specs = [pl.BlockSpec(memory_space=pltpu.SMEM), pl.BlockSpec(memory_space=pltpu.VMEM)]
    in_specs += [pl.BlockSpec(memory_space=pl.ANY)] * (len(args) - 2)
    some = depth * len(xs) * classes * width
    return pl.pallas_call(
        partial(body, xs),
        out_shape=out_shape,
        in_specs=in_specs,
        out_specs=jax.tree.map(lambda _: pl.BlockSpec(memory_space=pl.ANY), out_shape),
        scratch_shapes=scratch,
        input_output_aliases={len(args) - 1: 0} if into else {},
        compiler_params=pltpu.CompilerParams(vmem_limit_bytes=SETTLE_BYTES),
        cost_estimate=pl.CostEstimate(flops=12 * some, bytes_accessed=8 * some, transcendentals=some),
        name=name,
    )(*args)


def through_body(place_ref, flow_ref, marks_ref, rate_ref, through_ref):
    levels = flow_ref.shape[1]
    sources = marks_ref.shape[0]
    rows = through_ref.shape[0] // sources
    shape = through_ref.shape[1:]
    for source in range(sources):
        for x in range(rows):
            row = source * rows + x
            speed = marks_ref[source, x : x + 1, :] * jnp.broadcast_to(rate_ref[...], shape)
            bed = jnp.broadcast_to(marks_ref[source, rows + x : rows + x + 1, :], shape)
            through = jnp.ones(shape, F32)
            for k in range(levels):
                thick = flow_ref[0, k, row : row + 1, :]
                keep = speed * reciprocal(thick + speed)
                through = jnp.where(bed >= float(levels + k), through * keep, through)
            through_ref[row] = through


def near_body(place_ref, through_ref, own_ref, other_ref, near_ref):
    sources = own_ref.shape[0]
    classes = through_ref.shape[1]
    rows = through_ref.shape[0] // sources
    is_upper = place_ref[0] == 0
    for source in range(sources):
        for x in range(rows):
            part = slice(x * classes, (x + 1) * classes)
            own = own_ref[source, part, :]
            other = other_ref[source, part, :]
            upper = jnp.where(is_upper, own, other)
            lower = jnp.where(is_upper, other, own)
            near_ref[source * rows + x] = through_ref[source * rows + x] * upper + lower


def local(concentration, flow_planes, agg_kernel, settle_rate, wet_mask, bed_level):
    depth, rows, classes, width = concentration.shape
    planes, levels, tall, _ = flow_planes.shape
    groups, spread = lax.axis_size("lev"), lax.axis_size("horiz")
    lev, horiz = lax.axis_index("lev"), lax.axis_index("horiz")
    share = spread // groups
    place = jnp.stack([lev, horiz // share]).astype(jnp.int32)
    rate = settle_rate[:, None]

    slots = flow_planes.reshape(planes, groups, depth, share, rows, LANES).transpose(1, 3, 0, 2, 4, 5)
    slots = jnp.broadcast_to(slots[:, None], (groups, groups) + slots.shape[1:])
    slots = slots.reshape(groups * spread, planes * depth * rows, LANES)
    flow = lax.all_to_all(slots, ("lev", "horiz"), split_axis=0, concat_axis=0, tiled=True)

    tiles = 8
    change = change_of(pair_weights(agg_kernel, classes), concentration, tiles * LANES)

    operands = (concentration, change, flow, rate, wet_mask, bed_level)
    held = rows * classes
    marked = held + 8 * pl.cdiv(2 * rows, 8)
    slab = jax.ShapeDtypeStruct((spread, classes, LANES), F32)
    ahead = spread // 4
    flux_early, flux_ahead, flux_late, sent = settle_call(
        flux_body,
        (0, 1),
        "flux",
        place,
        operands,
        [],
        (
            slab,
            jax.ShapeDtypeStruct((ahead, classes, LANES), F32),
            jax.ShapeDtypeStruct((spread - ahead, classes, LANES), F32),
            jax.ShapeDtypeStruct((spread, marked, LANES), F32),
        ),
        lambda chunks, cols: [
            pltpu.VMEM((chunks, tiles, held, LANES), F32),
            pltpu.VMEM((chunks, tiles, marked - held, LANES), F32),
            pltpu.SemaphoreType.DMA((5, chunks)),
            pltpu.SemaphoreType.DMA((4, chunks)),
        ],
        tiles,
    )

    def beside(at):
        return at ^ BESIDE

    both = ("lev", "horiz")
    crossing = [(at, spread + beside(at)) for at in range(spread)]
    returning = [(spread + at, beside(at)) for at in range(spread)]
    swapping = [(spread + at, spread + beside(at)) for at in range(spread)]
    crossed = lax.ppermute(flux_early, both, crossing)
    crossed_ahead = lax.ppermute(flux_ahead, both, crossing)
    spread_out = lax.all_to_all(sent, "horiz", split_axis=0, concat_axis=0, tiled=True)
    crossed, flux_late = lax.optimization_barrier((crossed, flux_late))
    inflow_early = lax.ppermute(crossed, both, swapping)
    inflow_late = lax.ppermute(flux_late, "lev", [(0, 1)])
    inflow_ahead = lax.ppermute(crossed_ahead, both, swapping)
    away = lax.dynamic_slice(spread_out, ((1 - lev) * share, 0, 0), (share, held, LANES))
    other = lax.ppermute(away, both, crossing + returning)

    floc = []
    for x, inflow in ((0, (inflow_early,)), (1, (inflow_ahead, inflow_late))):
        floc = settle_call(
            partial(floc_body, len(inflow)),
            (x,),
            "floc",
            place,
            operands + inflow,
            floc,
            [jax.ShapeDtypeStruct(concentration.shape, BF16)],
            lambda chunks, cols: [
                pltpu.VMEM((chunks, depth, 1, classes, cols), BF16),
                pltpu.SemaphoreType.DMA((6, chunks)),
                pltpu.SemaphoreType.DMA((chunks,)),
            ],
            tiles,
        )
    floc = floc[0]

    near_shape = (tall, classes, LANES)
    some = 16
    steps = share // some
    near_block = pl.BlockSpec((some * rows, classes, LANES), lambda i, place: (i, 0, 0))
    through = pl.pallas_call(
        through_body,
        out_shape=jax.ShapeDtypeStruct(near_shape, F32),
        grid_spec=pltpu.PrefetchScalarGridSpec(
            num_scalar_prefetch=1,
            grid=(steps,),
            in_specs=[
                pl.BlockSpec((1, depth, some * rows, LANES), lambda i, place: (1, 1, i, 0)),
                pl.BlockSpec(
                    (some, marked - held, LANES),
                    lambda i, place: (place[0] * steps + i, held // (marked - held), 0),
                ),
                pl.BlockSpec(rate.shape, lambda i, place: (0, 0)),
            ],
            out_specs=near_block,
        ),
        compiler_params=pltpu.CompilerParams(vmem_limit_bytes=NEAR_BYTES),
        cost_estimate=pl.CostEstimate(
            flops=8 * depth * tall * classes * LANES,
            bytes_accessed=8 * tall * classes * LANES,
            transcendentals=depth * tall * classes * LANES,
        ),
        name="through",
    )(place, flow_planes, spread_out, rate)
    near_bed = pl.pallas_call(
        near_body,
        out_shape=jax.ShapeDtypeStruct(near_shape, F32),
        grid_spec=pltpu.PrefetchScalarGridSpec(
            num_scalar_prefetch=1,
            grid=(steps,),
            in_specs=[
                near_block,
                pl.BlockSpec((some, held, LANES), lambda i, place: (place[0] * steps + i, 0, 0)),
                pl.BlockSpec((some, held, LANES), lambda i, place: (i, 0, 0)),
            ],
            out_specs=near_block,
        ),
        compiler_params=pltpu.CompilerParams(vmem_limit_bytes=NEAR_BYTES),
        cost_estimate=pl.CostEstimate(
            flops=2 * tall * classes * LANES,
            bytes_accessed=16 * tall * classes * LANES,
            transcendentals=0,
        ),
        name="near",
    )(place, through, spread_out, other)
    return (floc, near_bed)


def solution(mesh):
    in_specs = (
        P("lev", "horiz", None, None),
        P(None, None, "lev", "horiz"),
        P(),
        P(),
        P("horiz", None),
        P("horiz", None),
    )
    out_specs = (P("lev", "horiz", None, None), P("lev", None, "horiz"))
    return jax.shard_map(local, mesh=mesh, in_specs=in_specs, out_specs=out_specs, check_vma=False)
```

```python
from functools import partial

import jax
import jax.numpy as jnp
import numpy as np
from jax import lax
from jax.experimental import pallas as pl
from jax.experimental.pallas import tpu as pltpu
from jax.sharding import PartitionSpec as P

LANES = 128
BESIDE = 8
F32 = jnp.float32
BF16 = jnp.bfloat16
VMEM_BYTES = 56 << 20
SETTLE_BYTES = 50 << 20
NEAR_BYTES = 16 << 20


def pair_order(classes):
    half = classes // 2
    order = [(one, half + two) for one in range(half) for two in range(half)]
    for base in (0, half):
        for shift in range(half // 2):
            order += [(base + one, base + (one + shift) % half) for one in range(half)]
    for base in (0, half):
        order += [(base + one, base + one + half // 2) for one in range(half // 2)]
    return order


def pair_weights(agg_kernel, classes):
    order = pair_order(classes)
    chosen = np.zeros((classes * classes, len(order)), np.float32)
    for place, (one, two) in enumerate(order):
        chosen[one * classes + two, place] = 1.0
        chosen[two * classes + one, place] = 1.0
    rows = lax.dot_general(
        agg_kernel, jnp.asarray(chosen, BF16), (((0,), (0,)), ((), ())), preferred_element_type=F32
    )
    high = lax.reduce_precision(rows, 8, 7)
    return jnp.concatenate([high, rows - high], axis=0).astype(BF16)


def pair_rows(conc):
    half = conc.shape[0] // 2
    quarter = half // 2
    halves = [conc[:half], conc[half:]]
    wide = [part.astype(F32) for part in halves]
    pairs = [
        halves[1] * jnp.broadcast_to(conc[one : one + 1], halves[1].shape) for one in range(half)
    ]
    for part, whole in zip(halves, wide):
        pairs.append(part * part)
        for shift in range(1, quarter):
            pairs.append(part * pltpu.roll(whole, half - shift, axis=0).astype(BF16))
    last = [whole[:quarter] * whole[quarter:] for whole in wide]
    pairs.append(jnp.concatenate(last, axis=0).astype(BF16))
    return jnp.concatenate(pairs, axis=0)


def change_body(step, weight_ref, conc_ref, change_ref):
    classes, width = conc_ref.shape[2:]
    cols = change_ref.shape[-1]
    for start in range(0, width, step):
        both = lax.dot_general(
            weight_ref[...],
            pair_rows(conc_ref[0, 0, :, start : start + step]),
            (((1,), (0,)), ((), ())),
            preferred_element_type=F32,
        )
        change = both[:classes] + both[classes:]
        for part in range(step // cols):
            change_ref[start // cols + part, 0, 0] = change[:, part * cols : (part + 1) * cols]


def change_of(weights, conc, cols):
    depth, rows, classes, width = conc.shape
    chunks = width // cols
    return pl.pallas_call(
        partial(change_body, 2 * cols),
        out_shape=jax.ShapeDtypeStruct((chunks, depth, rows, classes, cols), F32),
        grid=(depth, rows),
        in_specs=[
            pl.BlockSpec(weights.shape, lambda k, x: (0, 0)),
            pl.BlockSpec((1, 1, classes, width), lambda k, x: (k, x, 0, 0)),
        ],
        out_specs=pl.BlockSpec((chunks, 1, 1, classes, cols), lambda k, x: (0, k, x, 0, 0)),
        compiler_params=pltpu.CompilerParams(vmem_limit_bytes=VMEM_BYTES),
        cost_estimate=pl.CostEstimate(
            flops=2 * weights.size * depth * rows * width,
            bytes_accessed=6 * conc.size,
            transcendentals=0,
        ),
        name="change",
    )(weights, conc)


def reciprocal(x):
    return pl.reciprocal(x, approx=True)


def settle_block(xs, first_level, chunk, conc_ref, change_ref, flow_ref, rate_ref, wet_ref, bed_ref, start, emit):
    _, depth, _, classes, width = conc_ref.shape
    rows = wet_ref.shape[1]
    for tile in range(width // LANES):
        cols = slice(tile * LANES, (tile + 1) * LANES)
        for n, x in enumerate(xs):
            wet = wet_ref[chunk, x : x + 1, cols].astype(F32)
            bed = jnp.broadcast_to(bed_ref[chunk, x : x + 1, cols] - first_level, (classes, LANES))
            speed = wet * jnp.broadcast_to(rate_ref[...], (classes, LANES))
            carry = start(tile, n)
            for k in range(depth):
                shear = flow_ref[chunk, tile, k * rows + x : k * rows + x + 1, :]
                at = (depth + k) * rows + x
                thick = flow_ref[chunk, tile, at : at + 1, :]
                change = change_ref[chunk, k, n, :, cols]
                aggregated = conc_ref[chunk, k, n, :, cols].astype(F32) + (wet * shear) * change
                settled = (speed * carry + thick * aggregated) * reciprocal(thick + speed)
                above = k <= bed
                carry = jnp.where(above, settled, carry)
                emit(tile, n, k, above, carry)


def chunk_copies(xs, place_ref, hbm, held, sems, chunk):
    chunks = held[0].shape[0]
    width = held[0].shape[-1]
    tiles = held[2].shape[1]
    cols = pl.ds(chunk * width, width)
    some = pl.ds(xs[0], len(xs))
    parts = [
        hbm[0].at[:, some, :, cols],
        hbm[1].at[chunk, :, some],
        hbm[2].at[pl.ds(place_ref[1] * (chunks * tiles) + chunk * tiles, tiles)],
        hbm[3].at[:, cols],
        hbm[4].at[:, cols],
    ]
    if len(hbm) > 5:
        part, at = hbm[5], 0
        if isinstance(chunk, int):
            at = chunk * tiles
            for part in hbm[5:]:
                if at < part.shape[0]:
                    break
                at -= part.shape[0]
        parts.append(part.at[pl.ds(at, tiles)])
    return [
        pltpu.make_async_copy(part, held[at].at[chunk], sems.at[at, chunk])
        for at, part in enumerate(parts)
    ]


def flux_body(xs, place_ref, rate_ref, *refs):
    hbm, early_hbm, late_hbm, sent_hbm, held = refs[:5], refs[5], refs[6:8], refs[8], refs[9:14]
    value_ref, marks_ref, in_sems, out_sems = refs[14:]
    chunks, depth, rows, classes, _ = held[0].shape
    tiles = held[2].shape[1]
    for chunk in range(chunks):
        for copy in chunk_copies(xs, place_ref, hbm, held, in_sems, chunk):
            copy.start()
    zero = jnp.zeros((classes, LANES), F32)
    turned = jnp.where(place_ref[0] == place_ref[1], 0, 1)

    cut = late_hbm[0].shape[0] // tiles
    spans = ((0, cut), (cut, chunks))

    def sends(part, chunk):
        here = pl.ds(chunk * tiles, tiles)
        there = pl.ds((chunk - spans[part][0]) * tiles, tiles)
        to = pl.ds(jnp.bitwise_xor(chunk, turned) * tiles, tiles)
        top = rows * classes
        first, second = pl.ds(0, classes), pl.ds(classes, classes)
        return [
            pltpu.make_async_copy(value_ref.at[chunk, :, first], early_hbm.at[here], out_sems.at[0, chunk]),
            pltpu.make_async_copy(
                value_ref.at[chunk, :, second], late_hbm[part].at[there], out_sems.at[1, chunk]
            ),
            pltpu.make_async_copy(
                value_ref.at[chunk], sent_hbm.at[to, pl.ds(0, top)], out_sems.at[2, chunk]
            ),
            pltpu.make_async_copy(
                marks_ref.at[chunk], sent_hbm.at[to, pl.ds(top, marks_ref.shape[2])], out_sems.at[3, chunk]
            ),
        ]

    def step(part, chunk, _):
        for copy in chunk_copies(xs, place_ref, hbm, held, in_sems, chunk):
            copy.wait()

        def emit(tile, n, k, above, carry):
            if k == depth - 1:
                value_ref[chunk, tile, n * classes : (n + 1) * classes, :] = carry

        settle_block(
            xs, place_ref[0] * depth, chunk, *held[:3], rate_ref, *held[3:], lambda tile, n: zero, emit
        )
        for tile in range(tiles):
            cols = slice(tile * LANES, (tile + 1) * LANES)
            wet = held[3][chunk, :, cols].astype(F32)
            bed = held[4][chunk, :, cols].astype(F32)
            pad = jnp.zeros((marks_ref.shape[2] - 2 * rows, LANES), F32)
            marks_ref[chunk, tile] = jnp.concatenate([wet, bed, pad], axis=0)
        for copy in sends(part, chunk):
            copy.start()
        return 0

    for part, span in enumerate(spans):
        lax.fori_loop(*span, partial(step, part), 0)
    for part, span in enumerate(spans):
        for chunk in range(*span):
            for copy in sends(part, chunk):
                copy.wait()


def floc_body(parts, xs, place_ref, rate_ref, *refs):
    hbm, rest = refs[: 5 + parts], refs[-10:]
    floc_hbm, held = rest[0], rest[1:7]
    out_ref, in_sems, out_sems = rest[7:]
    chunks, depth, _, classes, width = held[0].shape
    for chunk in range(chunks):
        for copy in chunk_copies(xs, place_ref, hbm, held, in_sems, chunk):
            copy.start()

    def send(chunk):
        to = floc_hbm.at[:, pl.ds(xs[0], len(xs)), :, pl.ds(chunk * width, width)]
        return pltpu.make_async_copy(out_ref.at[chunk], to, out_sems.at[chunk])

    def step(chunk, _):
        for copy in chunk_copies(xs, place_ref, hbm, held, in_sems, chunk):
            copy.wait()

        def start(tile, n):
            return held[5][chunk, tile, n * classes : (n + 1) * classes, :]

        def emit(tile, n, k, above, carry):
            cols = slice(tile * LANES, (tile + 1) * LANES)
            out_ref[chunk, k, n, :, cols] = jnp.where(above, carry, 0.0).astype(BF16)

        settle_block(xs, place_ref[0] * depth, chunk, *held[:3], rate_ref, *held[3:5], start, emit)
        send(chunk).start()
        return 0

    lax.fori_loop(0, chunks, step, 0)
    for chunk in range(chunks):
        send(chunk).wait()


def settle_call(body, xs, name, place, operands, into, out_shape, extra_scratch, tiles):
    conc, change, flow, rate, wet, bed, *inflow = operands
    depth, rows, classes, width = conc.shape
    cols = tiles * LANES
    chunks = width // cols
    scratch = [
        pltpu.VMEM((chunks, depth, len(xs), classes, cols), BF16),
        pltpu.VMEM((chunks, depth, len(xs), classes, cols), F32),
        pltpu.VMEM((chunks, tiles) + flow.shape[1:], F32),
        pltpu.VMEM((chunks, rows, cols), jnp.int32),
        pltpu.VMEM((chunks, rows, cols), jnp.int32),
    ]
    if inflow:
        scratch.append(pltpu.VMEM((chunks, tiles) + inflow[0].shape[1:], F32))
    scratch += extra_scratch(chunks, cols)
    args = [place, rate, conc, change, flow, wet, bed, *inflow, *into]
    in_specs = [pl.BlockSpec(memory_space=pltpu.SMEM), pl.BlockSpec(memory_space=pltpu.VMEM)]
    in_specs += [pl.BlockSpec(memory_space=pl.ANY)] * (len(args) - 2)
    some = depth * len(xs) * classes * width
    return pl.pallas_call(
        partial(body, xs),
        out_shape=out_shape,
        in_specs=in_specs,
        out_specs=jax.tree.map(lambda _: pl.BlockSpec(memory_space=pl.ANY), out_shape),
        scratch_shapes=scratch,
        input_output_aliases={len(args) - 1: 0} if into else {},
        compiler_params=pltpu.CompilerParams(vmem_limit_bytes=SETTLE_BYTES),
        cost_estimate=pl.CostEstimate(flops=12 * some, bytes_accessed=8 * some, transcendentals=some),
        name=name,
    )(*args)


def through_body(place_ref, flow_ref, marks_ref, rate_ref, through_ref):
    levels = flow_ref.shape[1]
    sources = marks_ref.shape[0]
    rows = through_ref.shape[0] // sources
    shape = through_ref.shape[1:]
    for source in range(sources):
        for x in range(rows):
            row = source * rows + x
            speed = marks_ref[source, x : x + 1, :] * jnp.broadcast_to(rate_ref[...], shape)
            bed = jnp.broadcast_to(marks_ref[source, rows + x : rows + x + 1, :], shape)
            through = jnp.ones(shape, F32)
            for k in range(levels):
                thick = flow_ref[0, k, row : row + 1, :]
                keep = speed * reciprocal(thick + speed)
                through = jnp.where(bed >= float(levels + k), through * keep, through)
            through_ref[row] = through


def near_body(place_ref, through_ref, own_ref, other_ref, near_ref):
    sources = own_ref.shape[0]
    classes = through_ref.shape[1]
    rows = through_ref.shape[0] // sources
    is_upper = place_ref[0] == 0
    for source in range(sources):
        for x in range(rows):
            part = slice(x * classes, (x + 1) * classes)
            own = own_ref[source, part, :]
            other = other_ref[source, part, :]
            upper = jnp.where(is_upper, own, other)
            lower = jnp.where(is_upper, other, own)
            near_ref[source * rows + x] = through_ref[source * rows + x] * upper + lower


def local(concentration, flow_planes, agg_kernel, settle_rate, wet_mask, bed_level):
    depth, rows, classes, width = concentration.shape
    planes, levels, tall, _ = flow_planes.shape
    groups, spread = lax.axis_size("lev"), lax.axis_size("horiz")
    lev, horiz = lax.axis_index("lev"), lax.axis_index("horiz")
    share = spread // groups
    place = jnp.stack([lev, horiz // share]).astype(jnp.int32)
    rate = settle_rate[:, None]

    slots = flow_planes.reshape(planes, groups, depth, share, rows, LANES).transpose(1, 3, 0, 2, 4, 5)
    slots = jnp.broadcast_to(slots[:, None], (groups, groups) + slots.shape[1:])
    slots = slots.reshape(groups * spread, planes * depth * rows, LANES)
    flow = lax.all_to_all(slots, ("lev", "horiz"), split_axis=0, concat_axis=0, tiled=True)

    tiles = 8
    change = change_of(pair_weights(agg_kernel, classes), concentration, tiles * LANES)

    operands = (concentration, change, flow, rate, wet_mask, bed_level)
    held = rows * classes
    marked = held + 8 * pl.cdiv(2 * rows, 8)
    slab = jax.ShapeDtypeStruct((spread, classes, LANES), F32)
    ahead = spread // 4
    flux_early, flux_ahead, flux_late, sent = settle_call(
        flux_body,
        (0, 1),
        "flux",
        place,
        operands,
        [],
        (
            slab,
            jax.ShapeDtypeStruct((ahead, classes, LANES), F32),
            jax.ShapeDtypeStruct((spread - ahead, classes, LANES), F32),
            jax.ShapeDtypeStruct((spread, marked, LANES), F32),
        ),
        lambda chunks, cols: [
            pltpu.VMEM((chunks, tiles, held, LANES), F32),
            pltpu.VMEM((chunks, tiles, marked - held, LANES), F32),
            pltpu.SemaphoreType.DMA((5, chunks)),
            pltpu.SemaphoreType.DMA((4, chunks)),
        ],
        tiles,
    )

    def beside(at):
        return at ^ BESIDE

    both = ("lev", "horiz")
    crossing = [(at, spread + beside(at)) for at in range(spread)]
    returning = [(spread + at, beside(at)) for at in range(spread)]
    swapping = [(spread + at, spread + beside(at)) for at in range(spread)]
    crossed = lax.ppermute(flux_early, both, crossing)
    crossed_ahead = lax.ppermute(flux_ahead, both, crossing)
    spread_out = lax.all_to_all(sent, "horiz", split_axis=0, concat_axis=0, tiled=True)
    crossed, flux_late = lax.optimization_barrier((crossed, flux_late))
    spread_out, crossed_ahead = lax.optimization_barrier((spread_out, crossed_ahead))
    inflow_early = lax.ppermute(crossed, both, swapping)
    inflow_late = lax.ppermute(flux_late, "lev", [(0, 1)])
    inflow_ahead = lax.ppermute(crossed_ahead, both, swapping)
    away = lax.dynamic_slice(spread_out, ((1 - lev) * share, 0, 0), (share, held, LANES))
    other = lax.ppermute(away, both, crossing + returning)

    floc = []
    for x, inflow in ((0, (inflow_early,)), (1, (inflow_ahead, inflow_late))):
        floc = settle_call(
            partial(floc_body, len(inflow)),
            (x,),
            "floc",
            place,
            operands + inflow,
            floc,
            [jax.ShapeDtypeStruct(concentration.shape, BF16)],
            lambda chunks, cols: [
                pltpu.VMEM((chunks, depth, 1, classes, cols), BF16),
                pltpu.SemaphoreType.DMA((6, chunks)),
                pltpu.SemaphoreType.DMA((chunks,)),
            ],
            tiles,
        )
    floc = floc[0]

    near_shape = (tall, classes, LANES)
    some = 16
    steps = share // some
    near_block = pl.BlockSpec((some * rows, classes, LANES), lambda i, place: (i, 0, 0))
    through = pl.pallas_call(
        through_body,
        out_shape=jax.ShapeDtypeStruct(near_shape, F32),
        grid_spec=pltpu.PrefetchScalarGridSpec(
            num_scalar_prefetch=1,
            grid=(steps,),
            in_specs=[
                pl.BlockSpec((1, depth, some * rows, LANES), lambda i, place: (1, 1, i, 0)),
                pl.BlockSpec(
                    (some, marked - held, LANES),
                    lambda i, place: (place[0] * steps + i, held // (marked - held), 0),
                ),
                pl.BlockSpec(rate.shape, lambda i, place: (0, 0)),
            ],
            out_specs=near_block,
        ),
        compiler_params=pltpu.CompilerParams(vmem_limit_bytes=NEAR_BYTES),
        cost_estimate=pl.CostEstimate(
            flops=8 * depth * tall * classes * LANES,
            bytes_accessed=8 * tall * classes * LANES,
            transcendentals=depth * tall * classes * LANES,
        ),
        name="through",
    )(place, flow_planes, spread_out, rate)
    near_bed = pl.pallas_call(
        near_body,
        out_shape=jax.ShapeDtypeStruct(near_shape, F32),
        grid_spec=pltpu.PrefetchScalarGridSpec(
            num_scalar_prefetch=1,
            grid=(steps,),
            in_specs=[
                near_block,
                pl.BlockSpec((some, held, LANES), lambda i, place: (place[0] * steps + i, 0, 0)),
                pl.BlockSpec((some, held, LANES), lambda i, place: (i, 0, 0)),
            ],
            out_specs=near_block,
        ),
        compiler_params=pltpu.CompilerParams(vmem_limit_bytes=NEAR_BYTES),
        cost_estimate=pl.CostEstimate(
            flops=2 * tall * classes * LANES,
            bytes_accessed=16 * tall * classes * LANES,
            transcendentals=0,
        ),
        name="near",
    )(place, through, spread_out, other)
    return (floc, near_bed)


def solution(mesh):
    in_specs = (
        P("lev", "horiz", None, None),
        P(None, None, "lev", "horiz"),
        P(),
        P(),
        P("horiz", None),
        P("horiz", None),
    )
    out_specs = (P("lev", "horiz", None, None), P("lev", None, "horiz"))
    return jax.shard_map(local, mesh=mesh, in_specs=in_specs, out_specs=out_specs, check_vma=False)
```
